32 devices in a mesh: ctx: 8 (over z, x), head: 4 (over y, core).
Axes of the slice: x: 2, y: 2, z: 4, core: 2. Of those that a mesh axis runs over, the one named last changes fastest.
Arguments:
- lin_query: bfloat16 [2048, 256], P('ctx', 'head'), may hold values from -4 to 4
- lin_key: bfloat16 [2048, 256], P('ctx', 'head'), may hold values from -3 to 3
- lin_values: bfloat16 [2048, 2048], P('ctx', 'head'), may hold values from -43 to 43
- win_query: bfloat16 [2048, 2048], P('ctx', 'head'), may hold values from -30 to 30
- win_key: bfloat16 [2048, 2048], P('ctx', 'head'), may hold values from -30 to 30
- win_value: bfloat16 [2048, 2048], P('ctx', 'head'), may hold values from -4 to 4
- conv_weight: bfloat16 [3, 2048], P(None, 'head'), may hold values from -3 to 3
- head_gain: float32 [2048], P('head'), may hold values from 0.7 to 12.6
Outputs:
- mixed_out: bfloat16 [2048, 2048], P('ctx', 'head')
The draws below stay inside these ranges and needn't reach their ends.
All inputs are finite; a program needn't handle non-finite values.
Results may differ from the reference program's by a relative error of at most 0.0019.
Values may be sent and summed in bfloat16 or wider, within the bound.
A program may use at most 192 MiB of HBM per device.

```python
import math
import jax
import jax.numpy as jnp
from jax import lax

HEADS = 16
FDIM = 16
VDIM = 128
WIN = 64
TAPS = 3
TOK_DEV = 256
D = 2048
FEAT = 273
TOKENS = 2048


def window_pair(key):
    base = jax.random.fold_in(key, 404)
    query = jnp.clip(jax.random.normal(jax.random.fold_in(base, 1), (TOKENS, D), jnp.float32), -4.0, 4.0)
    keys = jnp.clip(jax.random.normal(jax.random.fold_in(base, 2), (TOKENS, D), jnp.float32), -4.0, 4.0)
    return (query.astype(jnp.bfloat16), keys.astype(jnp.bfloat16))


def draw_win_query(key, part):
    return window_pair(key)[0]


def draw_win_key(key, part):
    return window_pair(key)[1]


def linear_keys(key):
    base = jax.random.fold_in(key, 707)
    keys = jnp.clip(jax.random.normal(base, (TOKENS, HEADS * FDIM), jnp.float32), -3.0, 3.0)
    return keys.astype(jnp.bfloat16)


def draw_lin_key(key, part):
    return linear_keys(key)


def draw_lin_values(key, part):
    base = jax.random.fold_in(key, 505)
    keys = linear_keys(key).astype(jnp.float32)
    column = jnp.arange(D, dtype=jnp.int32)
    head_of = column // VDIM
    channel = column % VDIM
    first = head_of * FDIM + channel % FDIM
    second = head_of * FDIM + (channel // FDIM + channel + head_of) % FDIM
    product = keys[:, first] * keys[:, second]
    noise = jnp.clip(jax.random.normal(jax.random.fold_in(base, 1), (TOKENS, D), jnp.float32), -4.0, 4.0)
    offsets = 3.0 * jnp.clip(jax.random.normal(jax.random.fold_in(base, 2), (TOKENS // TOK_DEV, D), jnp.float32), -4.0, 4.0)
    rows = jnp.arange(TOKENS) // TOK_DEV
    return (3.0 * product + noise + offsets[rows]).astype(jnp.bfloat16)


def draw_head_gain(key, part):
    base = jax.random.fold_in(key, 606)
    ratio = 3.0
    column = jnp.arange(D).astype(jnp.float32)
    rising = jnp.exp(jnp.log(ratio) * column / (D - 1))
    jitter = jax.random.uniform(base, (D,), jnp.float32, 0.7, 1.4)
    return rising * jitter


def level_of(rng, shape, pieces, low, high):
    level, own = 1.0, jax.random.fold_in(rng, 6)
    for dim, shards_of in pieces:
        steps = jnp.exp(jax.random.uniform(jax.random.fold_in(own, dim), (shards_of,), jnp.float32, low / len(pieces), high / len(pieces)))
        level = level * jnp.repeat(steps, shape[dim] // shards_of).reshape([-1 if axis == dim else 1 for axis in range(len(shape))])
    return level


def scatter_about(stream_key, extent, spread, most, split=(), held_as=jnp.bfloat16):
    array = jax.random.normal(stream_key, extent, jnp.float32) * spread
    if len(split) > 0:
        array = level_of(stream_key, extent, split, -0.22, 0.18) * array
    return jnp.clip(array, min=-most, max=most).astype(held_as)


def setup_inputs(seed: int = 0) -> dict:
    key_list = jax.random.split(jax.random.key(seed), 9)
    lin_query = scatter_about(key_list[0], (TOKENS, HEADS * FDIM), 1.0, 4.0, ((0, 8), (1, 4)))
    lin_key = draw_lin_key(jax.random.fold_in(key_list[8], 71), 0)
    lin_values = draw_lin_values(jax.random.fold_in(key_list[8], 71), 0)
    win_query = draw_win_query(jax.random.fold_in(key_list[8], 71), 0)
    win_key = draw_win_key(jax.random.fold_in(key_list[8], 71), 0)
    win_value = scatter_about(key_list[5], (TOKENS, D), 1.0, 4.0, ((0, 8), (1, 4)))
    conv_weight = scatter_about(key_list[6], (TAPS, D), 0.6, 3.0, ((1, 4),))
    head_gain = draw_head_gain(jax.random.fold_in(key_list[8], 71), 0)
    return dict(lin_query=lin_query, lin_key=lin_key, lin_values=lin_values, win_query=win_query, win_key=win_key, win_value=win_value, conv_weight=conv_weight, head_gain=head_gain)


def features_outer(x_tok):
    xt = jnp.transpose(x_tok.astype(jnp.float32), (1, 2, 0))
    heads, fdim, count = xt.shape
    ones = jnp.ones((heads, 1, count), jnp.float32)
    outer = (xt[:, :, None, :] * xt[:, None, :, :]).reshape(heads, fdim * fdim, count) * (1.0 / math.sqrt(32.0))
    return jnp.concatenate([ones, xt * 0.5, outer], axis=1)

def window_slab(query, key_ext, value_ext, start):
    count, width = query.shape
    heads = width // VDIM
    blocks = count // WIN
    qb = query.astype(jnp.float32).reshape(blocks, WIN, heads, VDIM)
    prev_k = key_ext[:count].astype(jnp.float32).reshape(blocks, WIN, heads, VDIM)
    this_k = key_ext[WIN:].astype(jnp.float32).reshape(blocks, WIN, heads, VDIM)
    prev_v = value_ext[:count].astype(jnp.float32).reshape(blocks, WIN, heads, VDIM)
    this_v = value_ext[WIN:].astype(jnp.float32).reshape(blocks, WIN, heads, VDIM)
    keys = jnp.concatenate([prev_k, this_k], axis=1)
    vals = jnp.concatenate([prev_v, this_v], axis=1)
    scores = jnp.einsum('bihe,bjhe->bhij', qb, keys) * (1.0 / math.sqrt(VDIM))
    rows_i = jnp.arange(WIN, dtype=jnp.int32)[:, None]
    cols_j = jnp.arange(2 * WIN, dtype=jnp.int32)[None, :]
    block_ids = jnp.arange(blocks, dtype=jnp.int32)[:, None, None]
    position = start + block_ids * WIN + cols_j[None] - WIN
    allowed = (cols_j > rows_i)[None] & (cols_j <= rows_i + WIN)[None] & (position >= 0)
    allowed = allowed[:, None]
    top = lax.optimization_barrier(jnp.max(jnp.where(allowed, scores, jnp.float32(-1e+30)), axis=-1, keepdims=True))
    prob = jnp.where(allowed, jnp.exp(scores - top), jnp.float32(0.0))
    total = lax.optimization_barrier(jnp.sum(prob, axis=-1))
    prob_bf = lax.optimization_barrier(prob.astype(jnp.bfloat16)).astype(jnp.float32)
    out = jnp.einsum('bhij,bjhe->bihe', prob_bf, vals)
    out = out / jnp.transpose(total, (0, 2, 1))[..., None]
    return out.reshape(count, width)

def conv_slab(value_ext, weight, count):
    ext = value_ext.astype(jnp.float32)
    taps = weight.astype(jnp.float32)
    acc = jnp.zeros((count, ext.shape[1]), jnp.float32)
    for tap in range(TAPS):
        acc = acc + taps[tap][None, :] * ext[WIN - tap:WIN - tap + count]
    return acc

def reference(lin_query, lin_key, lin_values, win_query, win_key, win_value, conv_weight, head_gain):
    slabs = TOKENS // TOK_DEV
    pad_rows = jnp.zeros((WIN, D), jnp.bfloat16)
    key_pad = jnp.concatenate([pad_rows, win_key], axis=0)
    value_pad = jnp.concatenate([pad_rows, win_value], axis=0)
    gain = head_gain.astype(jnp.float32)

    def step(carry, slab):
        state, normer = carry
        begin = (slab * TOK_DEV).astype(jnp.int32)
        qs = lax.dynamic_slice_in_dim(lin_query, begin, TOK_DEV, 0).reshape(TOK_DEV, HEADS, FDIM)
        ks = lax.dynamic_slice_in_dim(lin_key, begin, TOK_DEV, 0).reshape(TOK_DEV, HEADS, FDIM)
        vs = lax.dynamic_slice_in_dim(lin_values, begin, TOK_DEV, 0).reshape(TOK_DEV, HEADS, VDIM)
        q32 = qs.astype(jnp.float32)
        k32 = ks.astype(jnp.float32)
        v32 = vs.astype(jnp.float32)
        sim = jnp.einsum('thf,shf->hts', q32, k32) * 0.25
        causal = jnp.arange(TOK_DEV, dtype=jnp.int32)[:, None] >= jnp.arange(TOK_DEV, dtype=jnp.int32)[None, :]
        weights = jnp.where(causal[None], 1.0 + sim + 0.5 * sim * sim, jnp.float32(0.0))
        inner_den = lax.optimization_barrier(jnp.sum(weights, axis=-1))
        weights_bf = lax.optimization_barrier(weights.astype(jnp.bfloat16)).astype(jnp.float32)
        inner_num = jnp.einsum('hts,shv->htv', weights_bf, v32)
        phi_q = features_outer(qs)
        phi_k = features_outer(ks)
        numer = inner_num + jnp.einsum('hft,hfv->htv', phi_q, state, precision=lax.Precision.HIGHEST)
        denom = inner_den + jnp.einsum('hft,hf->ht', phi_q, normer, precision=lax.Precision.HIGHEST)
        lin = jnp.transpose(numer / denom[..., None], (1, 0, 2)).reshape(TOK_DEV, D)
        state = state + jnp.einsum('hft,thv->hfv', phi_k, v32, precision=lax.Precision.HIGHEST)
        normer = normer + lax.optimization_barrier(jnp.sum(phi_k, axis=-1))
        wq = lax.dynamic_slice_in_dim(win_query, begin, TOK_DEV, 0)
        wk = lax.dynamic_slice_in_dim(key_pad, begin, TOK_DEV + WIN, 0)
        wv = lax.dynamic_slice_in_dim(value_pad, begin, TOK_DEV + WIN, 0)
        win = window_slab(wq, wk, wv, begin)
        conv = conv_slab(wv, conv_weight, TOK_DEV)
        mixed = gain[None, :] * (lin + win + conv)
        msq = lax.optimization_barrier(jnp.sum(mixed * mixed, axis=-1)) / D
        out = (mixed * lax.rsqrt(msq + 1e-06)[:, None]).astype(jnp.bfloat16)
        return ((state, normer), out)
    start_state = jnp.zeros((HEADS, FEAT, VDIM), jnp.float32)
    start_norm = jnp.zeros((HEADS, FEAT), jnp.float32)
    carry, outs = lax.scan(step, (start_state, start_norm), jnp.arange(slabs, dtype=jnp.int32))
    return outs.reshape(TOKENS, D)
```

```python
import functools

import jax
import jax.numpy as jnp
import numpy as np
from jax import lax
from jax.experimental import pallas as pl
from jax.experimental.pallas import tpu as pltpu
from jax.sharding import PartitionSpec as P

FDIM = 16
VDIM = 128
WIN = 64
TAPS = 3
BLK = 128
PAIRS = [(i, j) for i in range(FDIM) for j in range(i, FDIM)]
NP = len(PAIRS)
ONE = NP + FDIM
ROWS = ONE + 8
MESH = pl.DeviceIdType.MESH
F32 = jnp.float32
BF16 = jnp.bfloat16
NT = (((1,), (1,)), ((), ()))


def selectors(heads):
    first = np.zeros((FDIM, 256), np.float32)
    second_q = np.zeros((FDIM, 256), np.float32)
    second_k = np.zeros((FDIM, NP), np.float32)
    for f, (i, j) in enumerate(PAIRS):
        first[i, f] = 1.0
        second_k[j, f] = 1.0
        second_q[j, f] = 1.0 / 32.0 if i == j else 1.0 / 16.0
    for i in range(FDIM):
        first[i, NP + i] = 1.0
    rep = lambda a: np.tile(a, (heads, 1))
    return (
        jnp.asarray(rep(first), BF16),
        jnp.asarray(rep(second_q), BF16),
        jnp.asarray(rep(first[:, :ONE]).T, BF16),
        jnp.asarray(rep(second_k).T, BF16),
    )


def encode(x):
    tile = x[ONE:]
    keep = lax.broadcasted_iota(jnp.int32, tile.shape, 0) < 3
    hi = tile.astype(BF16).astype(F32)
    low = jnp.where(keep, tile - hi, 0.0)
    tile = jnp.where(keep, hi, 0.0) + pltpu.roll(low, 3, 0)
    return jnp.concatenate([x[:ONE], tile], axis=0).astype(BF16)


def decode(x):
    x = x.astype(F32)
    tile = x[ONE:]
    keep = lax.broadcasted_iota(jnp.int32, tile.shape, 0) < 3
    tile = jnp.where(keep, tile + pltpu.roll(tile, 5, 0), 0.0)
    return jnp.concatenate([x[:ONE], tile], axis=0)


def kernel(
    n, nh, heads, total_width,
    lq_ref, lk_ref, lv_ref, wq_ref, wk_ref, wv_ref, cw_ref, hg_ref, e1q_ref, e2q_ref, e1k_ref, e2k_ref,
    out_ref,
    own, zin, xin, fwd, hk, hv, mix, num, den, sq_out, sq_in,
    z_send, z_recv, x_send, x_recv, h_send, h_recv, s_send, s_recv,
):
    count = lq_ref.shape[0]
    ctx = lax.axis_index("ctx")
    hd = lax.axis_index("head")
    z = ctx // 2
    x = lax.rem(ctx, 2)
    nz = n // 2
    partner = ctx + 1 - 2 * x

    barrier = pltpu.get_barrier_semaphore()

    peers = jnp.minimum(ctx, 2) + jnp.minimum(n - 1 - ctx, 2) + (nh - 1)

    def greet(c, h):
        pl.semaphore_signal(barrier, inc=1, device_id=(c, h), device_id_type=MESH)

    for by in (-2, -1, 1, 2):
        @pl.when((ctx + by >= 0) & (ctx + by < n))
        def _(by=by):
            greet(ctx + by, hd)
    for j in range(1, nh):
        greet(ctx, lax.rem(hd + j, nh))

    lane_head = lax.broadcasted_iota(jnp.int32, (count, heads * FDIM), 1) // FDIM
    lk = lk_ref[...]
    lq = lq_ref[...]
    zero = jnp.zeros((), BF16)

    row8 = lax.broadcasted_iota(jnp.int32, (8, VDIM), 0)
    ones = jnp.ones((8, count), BF16)
    const = jnp.where(lax.broadcasted_iota(jnp.int32, (8, count), 0) == 0, 1.0, 0.0)
    for h in range(heads):
        kh = jnp.where(lane_head == h, lk, zero)
        a = lax.dot_general(e1k_ref[...], kh, NT, preferred_element_type=F32)
        b = lax.dot_general(e2k_ref[...], kh, NT, preferred_element_type=F32)
        phi = jnp.concatenate([a[:NP] * b, a[NP:], const], axis=0).astype(BF16)
        st = jnp.dot(phi, lv_ref[:, h * VDIM:(h + 1) * VDIM], preferred_element_type=F32)
        n_a = lax.dot_general(ones, phi[:VDIM], NT, preferred_element_type=F32)
        rest = jnp.concatenate([phi[VDIM:], jnp.zeros((2 * VDIM - ROWS, count), BF16)], axis=0)
        n_b = lax.dot_general(ones, rest, NT, preferred_element_type=F32)
        tile = st[ONE:] + jnp.where(row8 == 1, n_a, 0.0) + jnp.where(row8 == 2, n_b, 0.0)
        own[h] = jnp.concatenate([st[:ONE], tile], axis=0)

    pl.semaphore_wait(barrier, peers)

    def halo(src, dst, i):
        return pltpu.make_async_remote_copy(
            src_ref=src.at[pl.ds(count - WIN, WIN)], dst_ref=dst,
            send_sem=h_send.at[i], recv_sem=h_recv.at[i],
            device_id=(ctx + 1, hd), device_id_type=MESH)

    def z_copy(h):
        return pltpu.make_async_remote_copy(
            src_ref=fwd.at[h], dst_ref=zin.at[h], send_sem=z_send.at[h], recv_sem=z_recv.at[h],
            device_id=(ctx + 2, hd), device_id_type=MESH)

    def x_copy(h, src):
        return pltpu.make_async_remote_copy(
            src_ref=src.at[h], dst_ref=xin.at[h], send_sem=x_send.at[h], recv_sem=x_recv.at[h],
            device_id=(partner, hd), device_id_type=MESH)

    @pl.when(ctx < n - 1)
    def _():
        halo(wk_ref, hk, 0).start()
        halo(wv_ref, hv, 1).start()

    @pl.when(ctx == 0)
    def _():
        hk[...] = jnp.zeros_like(hk)
        hv[...] = jnp.zeros_like(hv)

    def send(h):
        @pl.when(z < nz - 1)
        def _():
            z_copy(h).start()

        @pl.when(x == 0)
        def _():
            x_copy(h, fwd).start()

    def first_chain():
        for h in range(heads):
            fwd[h] = encode(own[h])
            send(h)

    def chain():
        for h in range(heads):
            z_copy(h).wait_recv()

            @pl.when(x == 1)
            def _(h=h):
                x_copy(h, zin).start()

            fwd[h] = encode(decode(zin[h]) + own[h])
            send(h)

    pl.when(z == 0)(first_chain)
    pl.when(z == 1)(chain)

    row_i = lax.broadcasted_iota(jnp.int32, (count, count), 0)
    col_i = lax.broadcasted_iota(jnp.int32, (count, count), 1)
    causal = row_i >= col_i
    wr = lax.broadcasted_iota(jnp.int32, (BLK, BLK + WIN), 0)
    wc = lax.broadcasted_iota(jnp.int32, (BLK, BLK + WIN), 1)
    band = (wc > wr) & (wc <= wr + WIN)

    def inner(h):
        cols = slice(h * VDIM, (h + 1) * VDIM)
        kh = jnp.where(lane_head == h, lk, zero)
        s = lax.dot_general(lq, kh, NT, preferred_element_type=F32) * 0.25
        a = jnp.where(causal, 1.0 + s + 0.5 * s * s, 0.0)
        den[h] = jnp.sum(a, axis=-1, keepdims=True)
        num[:, cols] = jnp.dot(a.astype(BF16), lv_ref[:, cols], preferred_element_type=F32)

    def window(h, b, ext_k, ext_v, allowed):
        cols = slice(h * VDIM, (h + 1) * VDIM)
        rows = slice(b * BLK, (b + 1) * BLK)
        s = lax.dot_general(wq_ref[rows, cols], ext_k, NT, preferred_element_type=F32) * (1.0 / np.sqrt(VDIM))
        top = jnp.max(jnp.where(allowed, s, -1e30), axis=-1, keepdims=True)
        p = jnp.where(allowed, jnp.exp(s - top), 0.0)
        tot = jnp.sum(p, axis=-1, keepdims=True)
        o = jnp.dot(p.astype(BF16), ext_v, preferred_element_type=F32)
        mix[rows, cols] = o / tot

    def later_blocks(h):
        cols = slice(h * VDIM, (h + 1) * VDIM)
        for b in range(1, count // BLK):
            rows = slice(b * BLK - WIN, (b + 1) * BLK)
            window(h, b, wk_ref[rows, cols], wv_ref[rows, cols], band)

    def first_block(h):
        cols = slice(h * VDIM, (h + 1) * VDIM)
        ext_k = jnp.concatenate([hk[:, cols], wk_ref[:BLK, cols]], axis=0)
        ext_v = jnp.concatenate([hv[:, cols], wv_ref[:BLK, cols]], axis=0)
        window(h, 0, ext_k, ext_v, band & ((wc >= WIN) | (ctx > 0)))

    def conv(h):
        cols = slice(h * VDIM, (h + 1) * VDIM)
        ext = jnp.concatenate([hv[WIN - 16:, cols], wv_ref[:, cols]], axis=0).astype(F32)
        taps = cw_ref[:, cols].astype(F32)
        acc = taps[0:1] * ext[16:16 + count]
        for t in range(1, TAPS):
            acc = acc + taps[t:t + 1] * ext[16 - t:16 - t + count]
        mix[:, cols] += acc

    for h in range(heads):
        inner(h)
    pl.when(z == 2)(chain)
    for h in range(heads):
        later_blocks(h)

    @pl.when(ctx > 0)
    def _():
        halo(wk_ref, hk, 0).wait_recv()
        halo(wv_ref, hv, 1).wait_recv()

    for h in range(heads):
        first_block(h)
        conv(h)
    if nz > 3:
        pl.when(z > 2)(chain)

    lane = lax.broadcasted_iota(jnp.int32, (1, 256), 1)
    add1 = jnp.where(lane == ONE, 1.0, 0.0)
    add2 = jnp.where(lane == ONE, 1.0, jnp.where((lane >= NP) & (lane < ONE), 0.25, 0.0))
    squares = jnp.zeros((count, VDIM), F32)
    for h in range(heads):
        cols = slice(h * VDIM, (h + 1) * VDIM)
        qh = jnp.where(lane_head == h, lq, zero)
        a = jnp.dot(qh, e1q_ref[...], preferred_element_type=F32) + add1
        b = jnp.dot(qh, e2q_ref[...], preferred_element_type=F32) + add2
        phi = a * b

        @pl.when(ctx > 0)
        def _():
            x_copy(h, zin).wait_recv()

            @pl.when(z > 0)
            def _():
                own[h] = decode(zin[h]) + decode(xin[h])

            @pl.when(z == 0)
            def _():
                own[h] = decode(xin[h])

        @pl.when(ctx == 0)
        def _():
            own[h] = jnp.zeros((ROWS, VDIM), F32)

        st = own[h]
        tile = st[ONE:]
        norm = jnp.concatenate([tile[1:2], tile[2:3]], axis=1)
        state = jnp.concatenate([st[:ONE], jnp.zeros((8, VDIM), F32)], axis=0)
        phi_n = phi[:, :ROWS]
        p_hi = phi_n.astype(BF16)
        p_lo = (phi_n - p_hi.astype(F32)).astype(BF16)
        s_hi = state.astype(BF16)
        s_lo = (state - s_hi.astype(F32)).astype(BF16)
        cross = (
            jnp.dot(p_hi, s_hi, preferred_element_type=F32)
            + jnp.dot(p_hi, s_lo, preferred_element_type=F32)
            + jnp.dot(p_lo, s_hi, preferred_element_type=F32)
        )
        d = den[h] + jnp.sum(phi * norm, axis=-1, keepdims=True)
        lin = (num[:, cols] + cross + tile[0:1]) / d
        m = hg_ref[:, cols] * (lin + mix[:, cols])
        mix[:, cols] = m
        squares = squares + m * m

    row = jnp.sum(squares.T, axis=0, keepdims=True)
    sq_out[...] = jnp.broadcast_to(row, sq_out.shape)

    def sq_copy(j):
        return pltpu.make_async_remote_copy(
            src_ref=sq_out, dst_ref=sq_in.at[j - 1], send_sem=s_send.at[j - 1], recv_sem=s_recv.at[j - 1],
            device_id=(ctx, lax.rem(hd + j, nh)), device_id_type=MESH)

    for j in range(1, nh):
        sq_copy(j).start()
    tot = sq_out[...]
    for j in range(1, nh):
        sq_copy(j).wait_recv()
        tot = tot + sq_in[j - 1]
    scale = lax.rsqrt(tot * (1.0 / total_width) + 1e-6)
    scale = jnp.broadcast_to(scale[0:1], (VDIM, count)).T
    for h in range(heads):
        cols = slice(h * VDIM, (h + 1) * VDIM)
        out_ref[:, cols] = (mix[:, cols] * scale).astype(BF16)

    for j in range(1, nh):
        sq_copy(j).wait_send()

    @pl.when(ctx < n - 1)
    def _():
        halo(wk_ref, hk, 0).wait_send()
        halo(wv_ref, hv, 1).wait_send()

    for h in range(heads):
        @pl.when(z < nz - 1)
        def _(h=h):
            z_copy(h).wait_send()

        @pl.when((x == 0) | (z > 0))
        def _(h=h):
            x_copy(h, zin).wait_send()


def body(n, nh, lq, lk, lv, wq, wk, wv, cw, hg):
    count, width = wv.shape
    heads = width // VDIM
    vmem = pl.BlockSpec(memory_space=pltpu.VMEM)
    dma = pltpu.SemaphoreType.DMA
    call = pl.pallas_call(
        functools.partial(kernel, n, nh, heads, width * nh),
        out_shape=jax.ShapeDtypeStruct((count, width), BF16),
        in_specs=[vmem] * 12,
        out_specs=vmem,
        scratch_shapes=[
            pltpu.VMEM((heads, ROWS, VDIM), F32),
            pltpu.VMEM((heads, ROWS, VDIM), BF16),
            pltpu.VMEM((heads, ROWS, VDIM), BF16),
            pltpu.VMEM((heads, ROWS, VDIM), BF16),
            pltpu.VMEM((WIN, width), BF16),
            pltpu.VMEM((WIN, width), BF16),
            pltpu.VMEM((count, width), F32),
            pltpu.VMEM((count, width), F32),
            pltpu.VMEM((heads, count, 1), F32),
            pltpu.VMEM((8, count), F32),
            pltpu.VMEM((nh - 1, 8, count), F32),
            dma((heads,)), dma((heads,)), dma((heads,)), dma((heads,)),
            dma((2,)), dma((2,)), dma((nh - 1,)), dma((nh - 1,)),
        ],
        compiler_params=pltpu.CompilerParams(
            collective_id=0, has_side_effects=True, vmem_limit_bytes=40 * 1024 * 1024
        ),
        cost_estimate=pl.CostEstimate(flops=500_000_000, bytes_accessed=3_000_000, transcendentals=200_000),
    )
    return call(lq, lk, lv, wq, wk, wv, cw, hg.reshape(1, width), *selectors(heads))


def solution(mesh):
    both = P("ctx", "head")
    placed = (both, both, both, both, both, both, P(None, "head"), P("head"))
    return jax.shard_map(
        functools.partial(body, mesh.shape["ctx"], mesh.shape["head"]),
        mesh=mesh, in_specs=placed, out_specs=both, check_vma=False,
    )
```

```python
import functools

import jax
import jax.numpy as jnp
import numpy as np
from jax import lax
from jax.experimental import pallas as pl
from jax.experimental.pallas import tpu as pltpu
from jax.sharding import PartitionSpec as P

FDIM = 16
VDIM = 128
WIN = 64
TAPS = 3
BLK = 128
PAIRS = [(i, j) for i in range(FDIM) for j in range(i, FDIM)]
NP = len(PAIRS)
ONE = NP + FDIM
ROWS = ONE + 8
EK = ROWS + 144
MESH = pl.DeviceIdType.MESH
F32 = jnp.float32
BF16 = jnp.bfloat16
NT = (((1,), (1,)), ((), ()))


def selectors(heads):
    first = np.zeros((FDIM, 256), np.float32)
    second_q = np.zeros((FDIM, 256), np.float32)
    second_k = np.zeros((FDIM, NP), np.float32)
    for f, (i, j) in enumerate(PAIRS):
        first[i, f] = 1.0
        second_k[j, f] = 1.0
        second_q[j, f] = 1.0 / 32.0 if i == j else 1.0 / 16.0
    for i in range(FDIM):
        first[i, NP + i] = 1.0
    rep = lambda a: np.tile(a, (heads, 1))
    keys = np.zeros((EK, heads * FDIM), np.float32)
    keys[:ONE] = rep(first[:, :ONE]).T
    keys[ROWS:ROWS + NP] = rep(second_k).T
    return (
        jnp.asarray(np.concatenate([rep(f[:, c:c + VDIM]) for f in (first, second_q) for c in (0, VDIM)]), BF16),
        jnp.asarray(keys, BF16),
    )


def encode(x):
    tile = x[ONE:]
    keep = lax.broadcasted_iota(jnp.int32, tile.shape, 0) < 3
    hi = tile.astype(BF16).astype(F32)
    low = jnp.where(keep, tile - hi, 0.0)
    tile = jnp.where(keep, hi, 0.0) + pltpu.roll(low, 3, 0)
    return jnp.concatenate([x[:ONE], tile], axis=0).astype(BF16)


def decode(x):
    x = x.astype(F32)
    tile = x[ONE:]
    keep = lax.broadcasted_iota(jnp.int32, tile.shape, 0) < 3
    tile = jnp.where(keep, tile + pltpu.roll(tile, 5, 0), 0.0)
    return jnp.concatenate([x[:ONE], tile], axis=0)


def kernel(
    n, nh, heads, total_width,
    lq_hbm, lk_hbm, lv_hbm, wq_hbm, wk_hbm, wv_hbm, cw_hbm, hg_hbm, eq_hbm, ek_hbm,
    out_ref,
    lq_ref, lk_ref, lv_ref, wq_ref, wk_ref, wv_ref, cw_ref, hg_ref, eq_ref, ek_ref,
    own, zin, xin, fwd, hk, hv, mix, num, den, phq, sq_out, sq_in,
    in_sem, z_send, z_recv, x_send, x_recv, h_send, h_recv, s_send, s_recv,
):
    count = lv_ref.shape[0]
    ctx = lax.axis_index("ctx")
    hd = lax.axis_index("head")
    z = ctx // 2
    x = lax.rem(ctx, 2)
    nz = n // 2
    partner = ctx + 1 - 2 * x

    loads = {}
    for i, (name, src, dst) in enumerate([
        ("lk", lk_hbm, lk_ref), ("ek", ek_hbm, ek_ref), ("lv", lv_hbm, lv_ref),
        ("wk", wk_hbm, wk_ref), ("wv", wv_hbm, wv_ref), ("lq", lq_hbm, lq_ref),
        ("wq", wq_hbm, wq_ref), ("eq", eq_hbm, eq_ref), ("cw", cw_hbm, cw_ref), ("hg", hg_hbm, hg_ref),
    ]):
        loads[name] = pltpu.make_async_copy(src, dst, in_sem.at[i])
        loads[name].start()

    barrier = pltpu.get_barrier_semaphore()
    peers = jnp.minimum(ctx, 2) + jnp.minimum(n - 1 - ctx, 2) + (nh - 1)

    def greet(c, h):
        pl.semaphore_signal(barrier, inc=1, device_id=(c, h), device_id_type=MESH)

    for by in (-2, -1, 1, 2):
        @pl.when((ctx + by >= 0) & (ctx + by < n))
        def _(by=by):
            greet(ctx + by, hd)
    for j in range(1, nh):
        greet(ctx, lax.rem(hd + j, nh))

    def halo(src, dst, i):
        return pltpu.make_async_remote_copy(
            src_ref=src.at[pl.ds(count - WIN, WIN)], dst_ref=dst,
            send_sem=h_send.at[i], recv_sem=h_recv.at[i],
            device_id=(ctx + 1, hd), device_id_type=MESH)

    def z_copy(h):
        return pltpu.make_async_remote_copy(
            src_ref=fwd.at[h], dst_ref=zin.at[h], send_sem=z_send.at[h], recv_sem=z_recv.at[h],
            device_id=(ctx + 2, hd), device_id_type=MESH)

    def x_copy(h, src):
        return pltpu.make_async_remote_copy(
            src_ref=src.at[h], dst_ref=xin.at[h], send_sem=x_send.at[h], recv_sem=x_recv.at[h],
            device_id=(partner, hd), device_id_type=MESH)

    def send_halos():
        @pl.when(ctx < n - 1)
        def _():
            halo(wk_ref, hk, 0).start()
            halo(wv_ref, hv, 1).start()

    def send(h):
        @pl.when(z < nz - 1)
        def _():
            z_copy(h).start()

        @pl.when(x == 0)
        def _():
            x_copy(h, fwd).start()

    def chain(h):
        z_copy(h).wait_recv()

        @pl.when(x == 1)
        def _():
            x_copy(h, zin).start()

        fwd[h] = encode(decode(zin[h]) + own[h])
        send(h)

    row_head = lax.broadcasted_iota(jnp.int32, (heads * FDIM, count), 0) // FDIM
    zero = jnp.zeros((), BF16)
    row8 = lax.broadcasted_iota(jnp.int32, (8, VDIM), 0)
    ones = jnp.ones((8, count), BF16)
    const = jnp.where(lax.broadcasted_iota(jnp.int32, (8, count), 0) == 0, 1.0, 0.0)
    loads["lk"].wait()
    loads["ek"].wait()
    lk = lk_ref[...]
    phis = []
    for h in range(heads):
        kh = jnp.where(row_head == h, lk, zero)
        ab = jnp.dot(ek_ref[...], kh, preferred_element_type=F32)
        phis.append(jnp.concatenate(
            [ab[:NP] * ab[ROWS:ROWS + NP], ab[NP:ONE], const], axis=0).astype(BF16))
    loads["lv"].wait()
    for h in range(heads):
        phi = phis[h]
        st = jnp.dot(phi, lv_ref[:, h * VDIM:(h + 1) * VDIM], preferred_element_type=F32)
        n_a = lax.dot_general(ones, phi[:VDIM], NT, preferred_element_type=F32)
        rest = jnp.concatenate([phi[VDIM:], jnp.zeros((2 * VDIM - ROWS, count), BF16)], axis=0)
        n_b = lax.dot_general(ones, rest, NT, preferred_element_type=F32)
        tile = st[ONE:] + jnp.where(row8 == 1, n_a, 0.0) + jnp.where(row8 == 2, n_b, 0.0)
        own[h] = jnp.concatenate([st[:ONE], tile], axis=0)
        if h == 0:
            loads["wk"].wait()
            loads["wv"].wait()
            pl.semaphore_wait(barrier, peers)
            pl.when(z > 0)(send_halos)

        @pl.when(z == 0)
        def _(h=h):
            fwd[h] = encode(own[h])
            send(h)

    pl.when(z == 0)(send_halos)

    @pl.when(ctx == 0)
    def _():
        hk[...] = jnp.zeros_like(hk)
        hv[...] = jnp.zeros_like(hv)

    for name in ("lq", "wq", "eq", "cw", "hg"):
        loads[name].wait()
    lq = lq_ref[...].astype(F32).T.astype(BF16)
    causal = (lax.broadcasted_iota(jnp.int32, (BLK, BLK), 0)
              >= lax.broadcasted_iota(jnp.int32, (BLK, BLK), 1))
    wr = lax.broadcasted_iota(jnp.int32, (BLK, BLK + WIN), 0)
    wc = lax.broadcasted_iota(jnp.int32, (BLK, BLK + WIN), 1)
    band = (wc > wr) & (wc <= wr + WIN)
    lane = lax.broadcasted_iota(jnp.int32, (1, 256), 1)
    add1 = jnp.where(lane == ONE, 1.0, 0.0)
    add2 = jnp.where(lane == ONE, 1.0, jnp.where((lane >= NP) & (lane < ONE), 0.25, 0.0))
    eq_head = lax.broadcasted_iota(jnp.int32, (heads * FDIM, 512), 0) // FDIM

    fan = heads * FDIM
    eq = jnp.concatenate([eq_ref[k * fan:(k + 1) * fan] for k in range(4)], axis=1)

    def inner(h):
        cols = slice(h * VDIM, (h + 1) * VDIM)
        kh = jnp.where(row_head == h, lk, zero) * jnp.asarray(0.25, BF16)
        for b in range(count // BLK):
            rows = slice(b * BLK, (b + 1) * BLK)
            s = jnp.dot(lq[rows], kh[:, :(b + 1) * BLK], preferred_element_type=F32)
            a = 1.0 + s + 0.5 * s * s
            last = jnp.where(causal, a[:, b * BLK:], 0.0)
            a = last if b == 0 else jnp.concatenate([a[:, :b * BLK], last], axis=1)
            den[h, rows] = jnp.sum(a, axis=-1, keepdims=True)
            num[rows, cols] = jnp.dot(
                a.astype(BF16), lv_ref[:(b + 1) * BLK, cols], preferred_element_type=F32)

    def query_features(h):
        e = jnp.where(eq_head == h, eq, zero)
        ab = jnp.dot(lq, e, preferred_element_type=F32)
        phq[h] = ((ab[:, :256] + add1) * (ab[:, 256:] + add2)).astype(BF16)

    def window(h, b, ext_k, ext_v, allowed):
        cols = slice(h * VDIM, (h + 1) * VDIM)
        rows = slice(b * BLK, (b + 1) * BLK)
        s = lax.dot_general(wq_ref[rows, cols], ext_k, NT, preferred_element_type=F32) * (1.0 / np.sqrt(VDIM))
        top = jnp.max(jnp.where(allowed, s, -1e30), axis=-1, keepdims=True)
        p = jnp.where(allowed, jnp.exp(s - top), 0.0)
        tot = jnp.sum(p, axis=-1, keepdims=True)
        o = jnp.dot(p.astype(BF16), ext_v, preferred_element_type=F32)
        mix[rows, cols] = o * (1.0 / tot)

    def later_blocks(h):
        cols = slice(h * VDIM, (h + 1) * VDIM)
        for b in range(1, count // BLK):
            rows = slice(b * BLK - WIN, (b + 1) * BLK)
            window(h, b, wk_ref[rows, cols], wv_ref[rows, cols], band)

    def first_block_and_conv(h):
        if h == 0:
            @pl.when(ctx > 0)
            def _():
                halo(wk_ref, hk, 0).wait_recv()
                halo(wv_ref, hv, 1).wait_recv()

        cols = slice(h * VDIM, (h + 1) * VDIM)
        ext_k = jnp.concatenate([hk[:, cols], wk_ref[:BLK, cols]], axis=0)
        ext_v = jnp.concatenate([hv[:, cols], wv_ref[:BLK, cols]], axis=0)
        window(h, 0, ext_k, ext_v, band & ((wc >= WIN) | (ctx > 0)))
        ext = jnp.concatenate([hv[WIN - 16:, cols], wv_ref[:, cols]], axis=0).astype(F32)
        taps = cw_ref[:, cols].astype(F32)
        acc = taps[0:1] * ext[16:16 + count]
        for t in range(1, TAPS):
            acc = acc + taps[t:t + 1] * ext[16 - t:16 - t + count]
        mix[:, cols] = hg_ref[:, cols] * (mix[:, cols] + acc)

    units = [functools.partial(f, h)
             for f in (inner, query_features, later_blocks, first_block_and_conv)
             for h in range(heads)]
    slots = {}
    for level, begin in ((1, 2), (2, 6), (3, 10)):
        for h in range(heads):
            slots.setdefault(min(begin + 2 * h, len(units)), []).append((level, h))
    for u in range(len(units) + 1):
        for level, h in slots.get(u, []):
            here = z == level if level < 3 else z >= level
            pl.when(here)(functools.partial(chain, h))
        if u < len(units):
            units[u]()

    squares = jnp.zeros((count, VDIM), F32)
    for h in range(heads):
        cols = slice(h * VDIM, (h + 1) * VDIM)

        @pl.when(ctx > 0)
        def _():
            x_copy(h, zin).wait_recv()

            @pl.when(z > 0)
            def _():
                own[h] = decode(zin[h]) + decode(xin[h])

            @pl.when(z == 0)
            def _():
                own[h] = decode(xin[h])

        @pl.when(ctx == 0)
        def _():
            own[h] = jnp.zeros((ROWS, VDIM), F32)

        st = own[h]
        tile = st[ONE:]
        norm = jnp.concatenate([tile[1:2], tile[2:3]], axis=1)
        state = jnp.concatenate([st[:ONE], jnp.zeros((8, VDIM), F32)], axis=0).astype(BF16)
        cross = jnp.dot(phq[h][:, :ROWS], state, preferred_element_type=F32)
        d = den[h] + jnp.sum(phq[h].astype(F32) * norm, axis=-1, keepdims=True)
        lin = (num[:, cols] + cross + tile[0:1]) * (1.0 / d)
        m = hg_ref[:, cols] * lin + mix[:, cols]
        mix[:, cols] = m
        squares = squares + m * m

    row = jnp.sum(squares.T, axis=0, keepdims=True)
    sq_out[...] = jnp.broadcast_to(row, sq_out.shape)

    def sq_copy(j):
        return pltpu.make_async_remote_copy(
            src_ref=sq_out, dst_ref=sq_in.at[j - 1], send_sem=s_send.at[j - 1], recv_sem=s_recv.at[j - 1],
            device_id=(ctx, lax.rem(hd + j, nh)), device_id_type=MESH)

    for j in range(1, nh):
        sq_copy(j).start()
    tot = sq_out[...]
    for j in range(1, nh):
        sq_copy(j).wait_recv()
        tot = tot + sq_in[j - 1]
    scale = lax.rsqrt(tot * (1.0 / total_width) + 1e-6)
    scale = jnp.broadcast_to(scale[0:1], (VDIM, count)).T
    for h in range(heads):
        cols = slice(h * VDIM, (h + 1) * VDIM)
        out_ref[:, cols] = (mix[:, cols] * scale).astype(BF16)

    for j in range(1, nh):
        sq_copy(j).wait_send()

    @pl.when(ctx < n - 1)
    def _():
        halo(wk_ref, hk, 0).wait_send()
        halo(wv_ref, hv, 1).wait_send()

    for h in range(heads):
        @pl.when(z < nz - 1)
        def _(h=h):
            z_copy(h).wait_send()

        @pl.when((x == 0) | (z > 0))
        def _(h=h):
            x_copy(h, zin).wait_send()


def body(n, nh, lq, lk, lv, wq, wk, wv, cw, hg):
    count, width = wv.shape
    heads = width // VDIM
    vmem = pl.BlockSpec(memory_space=pltpu.VMEM)
    dma = pltpu.SemaphoreType.DMA
    call = pl.pallas_call(
        functools.partial(kernel, n, nh, heads, width * nh),
        out_shape=jax.ShapeDtypeStruct((count, width), BF16),
        in_specs=[pl.BlockSpec(memory_space=pltpu.HBM)] * 10,
        out_specs=vmem,
        scratch_shapes=[
            pltpu.VMEM(lq.shape[::-1], BF16),
            pltpu.VMEM(lk.shape[::-1], BF16),
            pltpu.VMEM((count, width), BF16),
            pltpu.VMEM((count, width), BF16),
            pltpu.VMEM((count, width), BF16),
            pltpu.VMEM((count, width), BF16),
            pltpu.VMEM(cw.shape, BF16),
            pltpu.VMEM((1, width), F32),
            pltpu.VMEM((4 * heads * FDIM, VDIM), BF16),
            pltpu.VMEM((EK, heads * FDIM), BF16),
            pltpu.VMEM((heads, ROWS, VDIM), F32),
            pltpu.VMEM((heads, ROWS, VDIM), BF16),
            pltpu.VMEM((heads, ROWS, VDIM), BF16),
            pltpu.VMEM((heads, ROWS, VDIM), BF16),
            pltpu.VMEM((WIN, width), BF16),
            pltpu.VMEM((WIN, width), BF16),
            pltpu.VMEM((count, width), F32),
            pltpu.VMEM((count, width), F32),
            pltpu.VMEM((heads, count, 1), F32),
            pltpu.VMEM((heads, count, 256), BF16),
            pltpu.VMEM((8, count), F32),
            pltpu.VMEM((nh - 1, 8, count), F32),
            dma((10,)), dma((heads,)), dma((heads,)), dma((heads,)), dma((heads,)),
            dma((2,)), dma((2,)), dma((nh - 1,)), dma((nh - 1,)),
        ],
        compiler_params=pltpu.CompilerParams(
            collective_id=0, has_side_effects=True, vmem_limit_bytes=60 * 1024 * 1024
        ),
        cost_estimate=pl.CostEstimate(flops=500_000_000, bytes_accessed=3_000_000, transcendentals=200_000),
    )
    return call(lq.T, lk.T, lv, wq, wk, wv, cw, hg.reshape(1, width), *selectors(heads))


def solution(mesh):
    both = P("ctx", "head")
    placed = (both, both, both, both, both, both, P(None, "head"), P("head"))
    return jax.shard_map(
        functools.partial(body, mesh.shape["ctx"], mesh.shape["head"]),
        mesh=mesh, in_specs=placed, out_specs=both, check_vma=False,
    )
```

```python
import functools

import jax
import jax.numpy as jnp
import numpy as np
from jax import lax
from jax.experimental import pallas as pl
from jax.experimental.pallas import tpu as pltpu
from jax.sharding import PartitionSpec as P

FDIM = 16
VDIM = 128
WIN = 64
TAPS = 3
BLK = 128
PAIRS = [(i, j) for i in range(FDIM) for j in range(i, FDIM)]
NP = len(PAIRS)
ONE = NP + FDIM
ROWS = ONE + 8
EK = ROWS + 144
MESH = pl.DeviceIdType.MESH
F32 = jnp.float32
BF16 = jnp.bfloat16
NT = (((1,), (1,)), ((), ()))


def selectors(heads):
    first = np.zeros((FDIM, 256), np.float32)
    second_q = np.zeros((FDIM, 256), np.float32)
    second_k = np.zeros((FDIM, NP), np.float32)
    for f, (i, j) in enumerate(PAIRS):
        first[i, f] = 1.0
        second_k[j, f] = 1.0
        second_q[j, f] = 1.0 / 32.0 if i == j else 1.0 / 16.0
    for i in range(FDIM):
        first[i, NP + i] = 1.0
    rep = lambda a: np.tile(a, (heads, 1))
    keys = np.zeros((EK, heads * FDIM), np.float32)
    keys[:ONE] = rep(first[:, :ONE]).T
    keys[ROWS:ROWS + NP] = rep(second_k).T
    return (
        jnp.asarray(np.concatenate([rep(f[:, c:c + VDIM]) for f in (first, second_q) for c in (0, VDIM)]), BF16),
        jnp.asarray(keys, BF16),
    )


def encode(x):
    tile = x[ONE:]
    keep = lax.broadcasted_iota(jnp.int32, tile.shape, 0) < 3
    hi = tile.astype(BF16).astype(F32)
    low = jnp.where(keep, tile - hi, 0.0)
    tile = jnp.where(keep, hi, 0.0) + pltpu.roll(low, 3, 0)
    return jnp.concatenate([x[:ONE], tile], axis=0).astype(BF16)


def decode(x):
    x = x.astype(F32)
    tile = x[ONE:]
    keep = lax.broadcasted_iota(jnp.int32, tile.shape, 0) < 3
    tile = jnp.where(keep, tile + pltpu.roll(tile, 5, 0), 0.0)
    return jnp.concatenate([x[:ONE], tile], axis=0)


def kernel(
    n, nh, heads, total_width,
    lq_hbm, lk_hbm, lv_hbm, wq_hbm, wk_hbm, wv_hbm, cw_hbm, hg_hbm, eq_hbm, ek_hbm,
    out_ref,
    lq_ref, lk_ref, lv_ref, wq_ref, wk_ref, wv_ref, cw_ref, hg_ref, eq_ref, ek_ref,
    own, zin, xin, fwd, hk, hv, mix, num, den, phq, sq_out, sq_in,
    in_sem, z_send, z_recv, x_send, x_recv, h_send, h_recv, s_send, s_recv,
):
    count = lv_ref.shape[0]
    ctx = lax.axis_index("ctx")
    hd = lax.axis_index("head")
    z = ctx // 2
    x = lax.rem(ctx, 2)
    nz = n // 2
    partner = ctx + 1 - 2 * x

    loads = {}
    for i, (name, src, dst) in enumerate([
        ("lk", lk_hbm, lk_ref), ("ek", ek_hbm, ek_ref), ("lv", lv_hbm, lv_ref),
        ("wk", wk_hbm, wk_ref), ("wv", wv_hbm, wv_ref), ("lq", lq_hbm, lq_ref),
        ("wq", wq_hbm, wq_ref), ("eq", eq_hbm, eq_ref), ("cw", cw_hbm, cw_ref), ("hg", hg_hbm, hg_ref),
    ]):
        loads[name] = pltpu.make_async_copy(src, dst, in_sem.at[i])
        loads[name].start()

    barrier = pltpu.get_barrier_semaphore()
    peers = jnp.minimum(ctx, 2) + jnp.minimum(n - 1 - ctx, 2) + (nh - 1)

    def greet(c, h):
        pl.semaphore_signal(barrier, inc=1, device_id=(c, h), device_id_type=MESH)

    for by in (-2, -1, 1, 2):
        @pl.when((ctx + by >= 0) & (ctx + by < n))
        def _(by=by):
            greet(ctx + by, hd)
    for j in range(1, nh):
        greet(ctx, lax.rem(hd + j, nh))

    def halo(src, dst, i):
        return pltpu.make_async_remote_copy(
            src_ref=src.at[pl.ds(count - WIN, WIN)], dst_ref=dst,
            send_sem=h_send.at[i], recv_sem=h_recv.at[i],
            device_id=(ctx + 1, hd), device_id_type=MESH)

    def z_copy(h):
        return pltpu.make_async_remote_copy(
            src_ref=fwd.at[h], dst_ref=zin.at[h], send_sem=z_send.at[h], recv_sem=z_recv.at[h],
            device_id=(ctx + 2, hd), device_id_type=MESH)

    def x_copy(h, src):
        return pltpu.make_async_remote_copy(
            src_ref=src.at[h], dst_ref=xin.at[h], send_sem=x_send.at[h], recv_sem=x_recv.at[h],
            device_id=(partner, hd), device_id_type=MESH)

    def send_halos():
        @pl.when(ctx < n - 1)
        def _():
            halo(wk_ref, hk, 0).start()
            halo(wv_ref, hv, 1).start()

    def send_z(h):
        @pl.when(z < nz - 1)
        def _():
            z_copy(h).start()

    def send_x(h):
        @pl.when(x == 0)
        def _():
            x_copy(h, fwd).start()

    def chain(h):
        z_copy(h).wait_recv()

        @pl.when(x == 1)
        def _():
            x_copy(h, zin).start()

        fwd[h] = encode(decode(zin[h]) + own[h])
        send_z(h)
        send_x(h)

    row_head = lax.broadcasted_iota(jnp.int32, (heads * FDIM, count), 0) // FDIM
    zero = jnp.zeros((), BF16)
    row8 = lax.broadcasted_iota(jnp.int32, (8, VDIM), 0)
    ones = jnp.ones((8, count), BF16)
    const = jnp.where(lax.broadcasted_iota(jnp.int32, (8, count), 0) == 0, 1.0, 0.0)
    loads["lk"].wait()
    loads["ek"].wait()
    lk = lk_ref[...]
    phis = []
    for h in range(heads):
        kh = jnp.where(row_head == h, lk, zero)
        ab = jnp.dot(ek_ref[...], kh, preferred_element_type=F32)
        phis.append(jnp.concatenate(
            [ab[:NP] * ab[ROWS:ROWS + NP], ab[NP:ONE], const], axis=0).astype(BF16))
    loads["lv"].wait()
    for h in range(heads):
        phi = phis[h]
        st = jnp.dot(phi, lv_ref[:, h * VDIM:(h + 1) * VDIM], preferred_element_type=F32)
        n_a = lax.dot_general(ones, phi[:VDIM], NT, preferred_element_type=F32)
        rest = jnp.concatenate([phi[VDIM:], jnp.zeros((2 * VDIM - ROWS, count), BF16)], axis=0)
        n_b = lax.dot_general(ones, rest, NT, preferred_element_type=F32)
        tile = st[ONE:] + jnp.where(row8 == 1, n_a, 0.0) + jnp.where(row8 == 2, n_b, 0.0)
        st = jnp.concatenate([st[:ONE], tile], axis=0)
        own[h] = st
        fwd[h] = encode(st)
        if h == min(1, heads - 1):
            loads["wk"].wait()
            loads["wv"].wait()
            pl.semaphore_wait(barrier, peers)

            @pl.when(z == 0)
            def _():
                for g in range(h):
                    send_z(g)

            pl.when((z > 0) | (x == 0))(send_halos)

            @pl.when(z == 0)
            def _():
                for g in range(h):
                    send_x(g)
        if h >= min(1, heads - 1):
            @pl.when(z == 0)
            def _(h=h):
                send_z(h)
                send_x(h)

    pl.when(ctx == 1)(send_halos)

    @pl.when(z == 0)
    def _():
        zin[...] = jnp.zeros_like(zin)

    @pl.when(ctx == 0)
    def _():
        hk[...] = jnp.zeros_like(hk)
        hv[...] = jnp.zeros_like(hv)
        xin[...] = jnp.zeros_like(xin)

    for name in ("lq", "wq", "eq", "cw", "hg"):
        loads[name].wait()
    lq = lq_ref[...].astype(F32).T.astype(BF16)
    causal = (lax.broadcasted_iota(jnp.int32, (BLK, BLK), 0)
              >= lax.broadcasted_iota(jnp.int32, (BLK, BLK), 1))
    wr = lax.broadcasted_iota(jnp.int32, (BLK, BLK + WIN), 0)
    wc = lax.broadcasted_iota(jnp.int32, (BLK, BLK + WIN), 1)
    band = (wc > wr) & (wc <= wr + WIN)
    lane = lax.broadcasted_iota(jnp.int32, (1, 256), 1)
    add1 = jnp.where(lane == ONE, 1.0, 0.0)
    add2 = jnp.where(lane == ONE, 1.0, jnp.where((lane >= NP) & (lane < ONE), 0.25, 0.0))
    eq_head = lax.broadcasted_iota(jnp.int32, (heads * FDIM, 512), 0) // FDIM

    fan = heads * FDIM
    eq = jnp.concatenate([eq_ref[k * fan:(k + 1) * fan] for k in range(4)], axis=1)

    def inner(h):
        cols = slice(h * VDIM, (h + 1) * VDIM)
        kh = jnp.where(row_head == h, lk, zero) * jnp.asarray(0.25, BF16)
        for b in range(count // BLK):
            rows = slice(b * BLK, (b + 1) * BLK)
            s = jnp.dot(lq[rows], kh[:, :(b + 1) * BLK], preferred_element_type=F32)
            a = 1.0 + s + 0.5 * s * s
            last = jnp.where(causal, a[:, b * BLK:], 0.0)
            a = last if b == 0 else jnp.concatenate([a[:, :b * BLK], last], axis=1)
            den[h, rows] = jnp.sum(a, axis=-1, keepdims=True)
            num[rows, cols] = jnp.dot(
                a.astype(BF16), lv_ref[:(b + 1) * BLK, cols], preferred_element_type=F32)

    def query_features(h):
        e = jnp.where(eq_head == h, eq, zero)
        ab = jnp.dot(lq, e, preferred_element_type=F32)
        phq[h] = ((ab[:, :256] + add1) * (ab[:, 256:] + add2)).astype(BF16)

    def window(h, b, ext_k, ext_v, allowed):
        cols = slice(h * VDIM, (h + 1) * VDIM)
        rows = slice(b * BLK, (b + 1) * BLK)
        s = lax.dot_general(wq_ref[rows, cols], ext_k, NT, preferred_element_type=F32) * (1.0 / np.sqrt(VDIM))
        top = jnp.max(jnp.where(allowed, s, -1e30), axis=-1, keepdims=True)
        p = jnp.where(allowed, jnp.exp(s - top), 0.0)
        tot = jnp.sum(p, axis=-1, keepdims=True)
        o = jnp.dot(p.astype(BF16), ext_v, preferred_element_type=F32)
        mix[rows, cols] = o * (1.0 / tot)

    def later_blocks(h):
        cols = slice(h * VDIM, (h + 1) * VDIM)
        for b in range(1, count // BLK):
            rows = slice(b * BLK - WIN, (b + 1) * BLK)
            window(h, b, wk_ref[rows, cols], wv_ref[rows, cols], band)

    def first_block_and_conv(h):
        cols = slice(h * VDIM, (h + 1) * VDIM)
        ext_k = jnp.concatenate([hk[:, cols], wk_ref[:BLK, cols]], axis=0)
        ext_v = jnp.concatenate([hv[:, cols], wv_ref[:BLK, cols]], axis=0)
        window(h, 0, ext_k, ext_v, band & ((wc >= WIN) | (ctx > 0)))
        ext = jnp.concatenate([hv[WIN - 16:, cols], wv_ref[:, cols]], axis=0).astype(F32)
        taps = cw_ref[:, cols].astype(F32)
        acc = taps[0:1] * ext[16:16 + count]
        for t in range(1, TAPS):
            acc = acc + taps[t:t + 1] * ext[16 - t:16 - t + count]
        mix[:, cols] = hg_ref[:, cols] * (mix[:, cols] + acc)

    def chain_all():
        for h in range(heads):
            chain(h)

    pl.when(z == 1)(chain_all)
    for h in range(heads):
        inner(h)
        query_features(h)
        later_blocks(h)
    pl.when(z == 2)(chain_all)

    @pl.when(ctx > 0)
    def _():
        halo(wk_ref, hk, 0).wait_recv()
        halo(wv_ref, hv, 1).wait_recv()

    for h in range(heads):
        first_block_and_conv(h)
    pl.when(z > 2)(chain_all)

    squares = jnp.zeros((count, VDIM), F32)
    for h in range(heads):
        cols = slice(h * VDIM, (h + 1) * VDIM)

        @pl.when(ctx > 0)
        def _():
            x_copy(h, zin).wait_recv()

        st = decode(zin[h]) + decode(xin[h])
        tile = st[ONE:]
        norm = jnp.concatenate([tile[1:2], tile[2:3]], axis=1)
        state = jnp.concatenate([st[:ONE], jnp.zeros((8, VDIM), F32)], axis=0).astype(BF16)
        cross = jnp.dot(phq[h][:, :ROWS], state, preferred_element_type=F32)
        d = den[h] + jnp.sum(phq[h].astype(F32) * norm, axis=-1, keepdims=True)
        lin = (num[:, cols] + cross + tile[0:1]) * (1.0 / d)
        m = hg_ref[:, cols] * lin + mix[:, cols]
        mix[:, cols] = m
        squares = squares + m * m

    row = jnp.sum(squares.T, axis=0, keepdims=True)
    sq_out[...] = jnp.broadcast_to(row, sq_out.shape)

    def sq_copy(j):
        return pltpu.make_async_remote_copy(
            src_ref=sq_out, dst_ref=sq_in.at[j - 1], send_sem=s_send.at[j - 1], recv_sem=s_recv.at[j - 1],
            device_id=(ctx, lax.rem(hd + j, nh)), device_id_type=MESH)

    for j in range(1, nh):
        sq_copy(j).start()
    tot = sq_out[...]
    for j in range(1, nh):
        sq_copy(j).wait_recv()
        tot = tot + sq_in[j - 1]
    scale = lax.rsqrt(tot * (1.0 / total_width) + 1e-6)
    scale = jnp.broadcast_to(scale[0:1], (VDIM, count)).T
    for h in range(heads):
        cols = slice(h * VDIM, (h + 1) * VDIM)
        out_ref[:, cols] = (mix[:, cols] * scale).astype(BF16)

    for j in range(1, nh):
        sq_copy(j).wait_send()

    @pl.when(ctx < n - 1)
    def _():
        halo(wk_ref, hk, 0).wait_send()
        halo(wv_ref, hv, 1).wait_send()

    for h in range(heads):
        @pl.when(z < nz - 1)
        def _(h=h):
            z_copy(h).wait_send()

        @pl.when((x == 0) | (z > 0))
        def _(h=h):
            x_copy(h, zin).wait_send()


def body(n, nh, lq, lk, lv, wq, wk, wv, cw, hg):
    count, width = wv.shape
    heads = width // VDIM
    vmem = pl.BlockSpec(memory_space=pltpu.VMEM)
    dma = pltpu.SemaphoreType.DMA
    call = pl.pallas_call(
        functools.partial(kernel, n, nh, heads, width * nh),
        out_shape=jax.ShapeDtypeStruct((count, width), BF16),
        in_specs=[pl.BlockSpec(memory_space=pltpu.HBM)] * 10,
        out_specs=vmem,
        scratch_shapes=[
            pltpu.VMEM(lq.shape[::-1], BF16),
            pltpu.VMEM(lk.shape[::-1], BF16),
            pltpu.VMEM((count, width), BF16),
            pltpu.VMEM((count, width), BF16),
            pltpu.VMEM((count, width), BF16),
            pltpu.VMEM((count, width), BF16),
            pltpu.VMEM(cw.shape, BF16),
            pltpu.VMEM((1, width), F32),
            pltpu.VMEM((4 * heads * FDIM, VDIM), BF16),
            pltpu.VMEM((EK, heads * FDIM), BF16),
            pltpu.VMEM((heads, ROWS, VDIM), F32),
            pltpu.VMEM((heads, ROWS, VDIM), BF16),
            pltpu.VMEM((heads, ROWS, VDIM), BF16),
            pltpu.VMEM((heads, ROWS, VDIM), BF16),
            pltpu.VMEM((WIN, width), BF16),
            pltpu.VMEM((WIN, width), BF16),
            pltpu.VMEM((count, width), F32),
            pltpu.VMEM((count, width), F32),
            pltpu.VMEM((heads, count, 1), F32),
            pltpu.VMEM((heads, count, 256), BF16),
            pltpu.VMEM((8, count), F32),
            pltpu.VMEM((nh - 1, 8, count), F32),
            dma((10,)), dma((heads,)), dma((heads,)), dma((heads,)), dma((heads,)),
            dma((2,)), dma((2,)), dma((nh - 1,)), dma((nh - 1,)),
        ],
        compiler_params=pltpu.CompilerParams(
            collective_id=0, has_side_effects=True, vmem_limit_bytes=54528 * 1024
        ),
        cost_estimate=pl.CostEstimate(flops=500_000_000, bytes_accessed=3_000_000, transcendentals=200_000),
    )
    return call(lq.T, lk.T, lv, wq, wk, wv, cw, hg.reshape(1, width), *selectors(heads))


def solution(mesh):
    both = P("ctx", "head")
    placed = (both, both, both, both, both, both, P(None, "head"), P("head"))
    return jax.shard_map(
        functools.partial(body, mesh.shape["ctx"], mesh.shape["head"]),
        mesh=mesh, in_specs=placed, out_specs=both, check_vma=False,
    )
```

```python
import functools

import jax
import jax.numpy as jnp
import numpy as np
from jax import lax
from jax.experimental import pallas as pl
from jax.experimental.pallas import tpu as pltpu
from jax.sharding import PartitionSpec as P

FDIM = 16
VDIM = 128
WIN = 64
TAPS = 3
BLK = 128
PAIRS = [(i, j) for i in range(FDIM) for j in range(i, FDIM)]
NP = len(PAIRS)
ONE = NP + FDIM
ROWS = ONE + 8
EK = ROWS + 144
HALF = ROWS // 2
MESH = pl.DeviceIdType.MESH
F32 = jnp.float32
BF16 = jnp.bfloat16
NT = (((1,), (1,)), ((), ()))


def selectors(heads):
    first = np.zeros((FDIM, 256), np.float32)
    second_q = np.zeros((FDIM, 256), np.float32)
    second_k = np.zeros((FDIM, NP), np.float32)
    for f, (i, j) in enumerate(PAIRS):
        first[i, f] = 1.0
        second_k[j, f] = 1.0
        second_q[j, f] = 1.0 / 32.0 if i == j else 1.0 / 16.0
    for i in range(FDIM):
        first[i, NP + i] = 1.0
    rep = lambda a: np.tile(a, (heads, 1))
    keys = np.zeros((EK, heads * FDIM), np.float32)
    keys[:ONE] = rep(first[:, :ONE]).T
    keys[ROWS:ROWS + NP] = rep(second_k).T
    return (
        jnp.asarray(np.concatenate([rep(f[:, c:c + VDIM]) for f in (first, second_q) for c in (0, VDIM)]), BF16),
        jnp.asarray(keys, BF16),
    )


def encode(x):
    tile = x[-8:]
    keep = lax.broadcasted_iota(jnp.int32, tile.shape, 0) < 3
    hi = tile.astype(BF16).astype(F32)
    low = jnp.where(keep, tile - hi, 0.0)
    tile = jnp.where(keep, hi, 0.0) + pltpu.roll(low, 3, 0)
    return jnp.concatenate([x[:-8], tile], axis=0).astype(BF16)


def decode(x):
    x = x.astype(F32)
    tile = x[-8:]
    keep = lax.broadcasted_iota(jnp.int32, tile.shape, 0) < 3
    tile = jnp.where(keep, tile + pltpu.roll(tile, 5, 0), 0.0)
    return jnp.concatenate([x[:-8], tile], axis=0)


def kernel(
    n, nh, heads, total_width,
    lq_hbm, lk_hbm, lv_hbm, wq_hbm, wk_hbm, wv_hbm, cw_hbm, hg_hbm, eq_hbm, ek_hbm,
    out_ref,
    lq_ref, lk_ref, lv_ref, wq_ref, wk_ref, wv_ref, cw_ref, hg_ref, eq_ref, ek_ref,
    own, zin, xin, fwd, hk, hv, mix, num, den, phq, sq_out, sq_in,
    in_sem, z_send, z_recv, x_send, x_recv, h_send, h_recv, s_send, s_recv,
):
    count = lv_ref.shape[0]
    ctx = lax.axis_index("ctx")
    hd = lax.axis_index("head")
    z = ctx // 2
    x = lax.rem(ctx, 2)
    nz = n // 2
    partner = ctx + 1 - 2 * x

    loads = {}
    for i, (name, src, dst) in enumerate([
        ("lk", lk_hbm, lk_ref), ("ek", ek_hbm, ek_ref), ("lv", lv_hbm, lv_ref),
        ("wk", wk_hbm, wk_ref), ("wv", wv_hbm, wv_ref), ("lq", lq_hbm, lq_ref),
        ("wq", wq_hbm, wq_ref), ("eq", eq_hbm, eq_ref), ("cw", cw_hbm, cw_ref), ("hg", hg_hbm, hg_ref),
    ]):
        loads[name] = pltpu.make_async_copy(src, dst, in_sem.at[i])
        loads[name].start()

    barrier = pltpu.get_barrier_semaphore()
    peers = jnp.minimum(ctx, 2) + jnp.minimum(n - 1 - ctx, 2) + (nh - 1)

    def greet(c, h):
        pl.semaphore_signal(barrier, inc=1, device_id=(c, h), device_id_type=MESH)

    for by in (-2, -1, 1, 2):
        @pl.when((ctx + by >= 0) & (ctx + by < n))
        def _(by=by):
            greet(ctx + by, hd)
    for j in range(1, nh):
        greet(ctx, lax.rem(hd + j, nh))

    def halo(src, dst, i):
        return pltpu.make_async_remote_copy(
            src_ref=src.at[pl.ds(count - WIN, WIN)], dst_ref=dst,
            send_sem=h_send.at[i], recv_sem=h_recv.at[i],
            device_id=(ctx + 1, hd), device_id_type=MESH)

    def part(ref, c):
        return ref.at[c // 2, pl.ds(c % 2 * HALF, HALF)]

    def z_copy(c):
        return pltpu.make_async_remote_copy(
            src_ref=part(fwd, c), dst_ref=part(zin, c), send_sem=z_send.at[c], recv_sem=z_recv.at[c],
            device_id=(ctx + 2, hd), device_id_type=MESH)

    def x_copy(c, src):
        return pltpu.make_async_remote_copy(
            src_ref=part(src, c), dst_ref=part(xin, c), send_sem=x_send.at[c], recv_sem=x_recv.at[c],
            device_id=(partner, hd), device_id_type=MESH)

    def send_halos():
        @pl.when(ctx < n - 1)
        def _():
            halo(wk_ref, hk, 0).start()
            halo(wv_ref, hv, 1).start()

    def send_z(h):
        @pl.when(z < nz - 1)
        def _():
            z_copy(2 * h).start()
            z_copy(2 * h + 1).start()

    def send_x(h):
        @pl.when(x == 0)
        def _():
            x_copy(2 * h, fwd).start()
            x_copy(2 * h + 1, fwd).start()

    def chain(c):
        h, rows = c // 2, slice(c % 2 * HALF, (c % 2 + 1) * HALF)
        z_copy(c).wait_recv()

        @pl.when(x == 1)
        def _():
            x_copy(c, zin).start()

        if c % 2:
            fwd[h, rows] = encode(decode(zin[h, rows]) + own[h, rows])
        else:
            fwd[h, rows] = (zin[h, rows].astype(F32) + own[h, rows]).astype(BF16)

        @pl.when(z < nz - 1)
        def _():
            z_copy(c).start()

        @pl.when(x == 0)
        def _():
            x_copy(c, fwd).start()

    row_head = lax.broadcasted_iota(jnp.int32, (heads * FDIM, count), 0) // FDIM
    zero = jnp.zeros((), BF16)
    row8 = lax.broadcasted_iota(jnp.int32, (8, VDIM), 0)
    ones = jnp.ones((8, count), BF16)
    const = jnp.where(lax.broadcasted_iota(jnp.int32, (8, count), 0) == 0, 1.0, 0.0)
    loads["lk"].wait()
    loads["ek"].wait()
    lk = lk_ref[...]
    phis = []
    for h in range(heads):
        kh = jnp.where(row_head == h, lk, zero)
        ab = jnp.dot(ek_ref[...], kh, preferred_element_type=F32)
        phis.append(jnp.concatenate(
            [ab[:NP] * ab[ROWS:ROWS + NP], ab[NP:ONE], const], axis=0).astype(BF16))
    loads["lv"].wait()
    for h in range(heads):
        phi = phis[h]
        st = jnp.dot(phi, lv_ref[:, h * VDIM:(h + 1) * VDIM], preferred_element_type=F32)
        n_a = lax.dot_general(ones, phi[:VDIM], NT, preferred_element_type=F32)
        rest = jnp.concatenate([phi[VDIM:], jnp.zeros((2 * VDIM - ROWS, count), BF16)], axis=0)
        n_b = lax.dot_general(ones, rest, NT, preferred_element_type=F32)
        tile = st[ONE:] + jnp.where(row8 == 1, n_a, 0.0) + jnp.where(row8 == 2, n_b, 0.0)
        st = jnp.concatenate([st[:ONE], tile], axis=0)
        own[h] = st
        fwd[h] = encode(st)
        if h == min(1, heads - 1):
            loads["wk"].wait()
            loads["wv"].wait()
            pl.semaphore_wait(barrier, peers)

            @pl.when(z == 0)
            def _():
                for g in range(h):
                    send_z(g)

            pl.when((z > 0) | (x == 0))(send_halos)

            @pl.when(z == 0)
            def _():
                for g in range(h):
                    send_x(g)
        if h >= min(1, heads - 1):
            @pl.when(z == 0)
            def _(h=h):
                send_z(h)
                send_x(h)

    pl.when(ctx == 1)(send_halos)

    @pl.when(z == 0)
    def _():
        zin[...] = jnp.zeros_like(zin)

    @pl.when(ctx == 0)
    def _():
        hk[...] = jnp.zeros_like(hk)
        hv[...] = jnp.zeros_like(hv)
        xin[...] = jnp.zeros_like(xin)

    for name in ("lq", "wq", "eq", "cw", "hg"):
        loads[name].wait()
    lq = lq_ref[...].astype(F32).T.astype(BF16)
    causal = (lax.broadcasted_iota(jnp.int32, (BLK, BLK), 0)
              >= lax.broadcasted_iota(jnp.int32, (BLK, BLK), 1))
    wr = lax.broadcasted_iota(jnp.int32, (BLK, BLK + WIN), 0)
    wc = lax.broadcasted_iota(jnp.int32, (BLK, BLK + WIN), 1)
    band = (wc > wr) & (wc <= wr + WIN)
    lane = lax.broadcasted_iota(jnp.int32, (1, 256), 1)
    add1 = jnp.where(lane == ONE, 1.0, 0.0)
    add2 = jnp.where(lane == ONE, 1.0, jnp.where((lane >= NP) & (lane < ONE), 0.25, 0.0))
    eq_head = lax.broadcasted_iota(jnp.int32, (heads * FDIM, 512), 0) // FDIM

    fan = heads * FDIM
    eq = jnp.concatenate([eq_ref[k * fan:(k + 1) * fan] for k in range(4)], axis=1)

    def inner(h):
        cols = slice(h * VDIM, (h + 1) * VDIM)
        kh = jnp.where(row_head == h, lk, zero) * jnp.asarray(0.25, BF16)
        for b in range(count // BLK):
            rows = slice(b * BLK, (b + 1) * BLK)
            s = jnp.dot(lq[rows], kh[:, :(b + 1) * BLK], preferred_element_type=F32)
            a = 1.0 + s + 0.5 * s * s
            last = jnp.where(causal, a[:, b * BLK:], 0.0)
            a = last if b == 0 else jnp.concatenate([a[:, :b * BLK], last], axis=1)
            den[h, rows] = jnp.sum(a, axis=-1, keepdims=True)
            num[rows, cols] = jnp.dot(
                a.astype(BF16), lv_ref[:(b + 1) * BLK, cols], preferred_element_type=F32)

    def query_features(h):
        e = jnp.where(eq_head == h, eq, zero)
        ab = jnp.dot(lq, e, preferred_element_type=F32)
        phq[h] = ((ab[:, :256] + add1) * (ab[:, 256:] + add2)).astype(BF16)

    def window(h, b, ext_k, ext_v, allowed):
        cols = slice(h * VDIM, (h + 1) * VDIM)
        rows = slice(b * BLK, (b + 1) * BLK)
        s = lax.dot_general(wq_ref[rows, cols], ext_k, NT, preferred_element_type=F32) * (1.0 / np.sqrt(VDIM))
        top = jnp.max(jnp.where(allowed, s, -1e30), axis=-1, keepdims=True)
        p = jnp.where(allowed, jnp.exp(s - top), 0.0)
        tot = jnp.sum(p, axis=-1, keepdims=True)
        o = jnp.dot(p.astype(BF16), ext_v, preferred_element_type=F32)
        mix[rows, cols] = o * (1.0 / tot)

    def later_blocks(h):
        cols = slice(h * VDIM, (h + 1) * VDIM)
        for b in range(1, count // BLK):
            rows = slice(b * BLK - WIN, (b + 1) * BLK)
            window(h, b, wk_ref[rows, cols], wv_ref[rows, cols], band)

    def first_block_and_conv(h):
        cols = slice(h * VDIM, (h + 1) * VDIM)
        ext_k = jnp.concatenate([hk[:, cols], wk_ref[:BLK, cols]], axis=0)
        ext_v = jnp.concatenate([hv[:, cols], wv_ref[:BLK, cols]], axis=0)
        window(h, 0, ext_k, ext_v, band & ((wc >= WIN) | (ctx > 0)))
        ext = jnp.concatenate([hv[WIN - 16:, cols], wv_ref[:, cols]], axis=0).astype(F32)
        taps = cw_ref[:, cols].astype(F32)
        acc = taps[0:1] * ext[16:16 + count]
        for t in range(1, TAPS):
            acc = acc + taps[t:t + 1] * ext[16 - t:16 - t + count]
        mix[:, cols] = hg_ref[:, cols] * (mix[:, cols] + acc)

    def chain_all():
        for c in range(2 * heads):
            chain(c)

    pl.when(z == 1)(chain_all)
    for h in range(heads):
        inner(h)
        query_features(h)
        later_blocks(h)
    pl.when(z == 2)(chain_all)

    @pl.when(ctx > 0)
    def _():
        halo(wk_ref, hk, 0).wait_recv()
        halo(wv_ref, hv, 1).wait_recv()

    for h in range(heads):
        first_block_and_conv(h)
    pl.when(z > 2)(chain_all)

    squares = jnp.zeros((count, VDIM), F32)
    for h in range(heads):
        cols = slice(h * VDIM, (h + 1) * VDIM)

        @pl.when(ctx > 0)
        def _():
            x_copy(2 * h, zin).wait_recv()
            x_copy(2 * h + 1, zin).wait_recv()

        st = decode(zin[h]) + decode(xin[h])
        tile = st[ONE:]
        norm = jnp.concatenate([tile[1:2], tile[2:3]], axis=1)
        state = jnp.concatenate([st[:ONE], jnp.zeros((8, VDIM), F32)], axis=0).astype(BF16)
        cross = jnp.dot(phq[h][:, :ROWS], state, preferred_element_type=F32)
        d = den[h] + jnp.sum(phq[h].astype(F32) * norm, axis=-1, keepdims=True)
        lin = (num[:, cols] + cross + tile[0:1]) * (1.0 / d)
        m = hg_ref[:, cols] * lin + mix[:, cols]
        mix[:, cols] = m
        squares = squares + m * m

    row = jnp.sum(squares.T, axis=0, keepdims=True)
    sq_out[...] = jnp.broadcast_to(row, sq_out.shape)

    def sq_copy(j):
        return pltpu.make_async_remote_copy(
            src_ref=sq_out, dst_ref=sq_in.at[j - 1], send_sem=s_send.at[j - 1], recv_sem=s_recv.at[j - 1],
            device_id=(ctx, lax.rem(hd + j, nh)), device_id_type=MESH)

    for j in range(1, nh):
        sq_copy(j).start()
    tot = sq_out[...]
    for j in range(1, nh):
        sq_copy(j).wait_recv()
        tot = tot + sq_in[j - 1]
    scale = lax.rsqrt(tot * (1.0 / total_width) + 1e-6)
    scale = jnp.broadcast_to(scale[0:1], (VDIM, count)).T
    for h in range(heads):
        cols = slice(h * VDIM, (h + 1) * VDIM)
        out_ref[:, cols] = (mix[:, cols] * scale).astype(BF16)

    for j in range(1, nh):
        sq_copy(j).wait_send()

    @pl.when(ctx < n - 1)
    def _():
        halo(wk_ref, hk, 0).wait_send()
        halo(wv_ref, hv, 1).wait_send()

    for c in range(2 * heads):
        @pl.when(z < nz - 1)
        def _(c=c):
            z_copy(c).wait_send()

        @pl.when((x == 0) | (z > 0))
        def _(c=c):
            x_copy(c, zin).wait_send()


def body(n, nh, lq, lk, lv, wq, wk, wv, cw, hg):
    count, width = wv.shape
    heads = width // VDIM
    vmem = pl.BlockSpec(memory_space=pltpu.VMEM)
    dma = pltpu.SemaphoreType.DMA
    call = pl.pallas_call(
        functools.partial(kernel, n, nh, heads, width * nh),
        out_shape=jax.ShapeDtypeStruct((count, width), BF16),
        in_specs=[pl.BlockSpec(memory_space=pltpu.HBM)] * 10,
        out_specs=vmem,
        scratch_shapes=[
            pltpu.VMEM(lq.shape[::-1], BF16),
            pltpu.VMEM(lk.shape[::-1], BF16),
            pltpu.VMEM((count, width), BF16),
            pltpu.VMEM((count, width), BF16),
            pltpu.VMEM((count, width), BF16),
            pltpu.VMEM((count, width), BF16),
            pltpu.VMEM(cw.shape, BF16),
            pltpu.VMEM((1, width), F32),
            pltpu.VMEM((4 * heads * FDIM, VDIM), BF16),
            pltpu.VMEM((EK, heads * FDIM), BF16),
            pltpu.VMEM((heads, ROWS, VDIM), F32),
            pltpu.VMEM((heads, ROWS, VDIM), BF16),
            pltpu.VMEM((heads, ROWS, VDIM), BF16),
            pltpu.VMEM((heads, ROWS, VDIM), BF16),
            pltpu.VMEM((WIN, width), BF16),
            pltpu.VMEM((WIN, width), BF16),
            pltpu.VMEM((count, width), F32),
            pltpu.VMEM((count, width), F32),
            pltpu.VMEM((heads, count, 1), F32),
            pltpu.VMEM((heads, count, 256), BF16),
            pltpu.VMEM((8, count), F32),
            pltpu.VMEM((nh - 1, 8, count), F32),
            dma((10,)), dma((2 * heads,)), dma((2 * heads,)), dma((2 * heads,)), dma((2 * heads,)),
            dma((2,)), dma((2,)), dma((nh - 1,)), dma((nh - 1,)),
        ],
        compiler_params=pltpu.CompilerParams(
            collective_id=0, has_side_effects=True, vmem_limit_bytes=60 * 1024 * 1024
        ),
        cost_estimate=pl.CostEstimate(flops=500_000_000, bytes_accessed=3_000_000, transcendentals=200_000),
    )
    return call(lq.T, lk.T, lv, wq, wk, wv, cw, hg.reshape(1, width), *selectors(heads))


def solution(mesh):
    both = P("ctx", "head")
    placed = (both, both, both, both, both, both, P(None, "head"), P("head"))
    return jax.shard_map(
        functools.partial(body, mesh.shape["ctx"], mesh.shape["head"]),
        mesh=mesh, in_specs=placed, out_specs=both, check_vma=False,
    )
```
